32 devices in a mesh: ctx: 16 (over z, x, core), head: 2 (over y).
Axes of the slice: x: 2, y: 2, z: 4, core: 2. Of those that a mesh axis runs over, the one named last changes fastest.
Arguments:
- queries: bfloat16 [8192, 2048], P('ctx', 'head'), may hold values from -24 to 24
- keys: bfloat16 [8192, 1024], P('ctx', 'head'), may hold values from -6 to 6
- values: bfloat16 [8192, 1024], P('ctx', 'head'), may hold values from -6 to 6
- out_weight: bfloat16 [128, 16, 4608], P(None, 'head'), may hold values from -0.125 to 0.125
- cotangent: bfloat16 [8192, 4608], P(('ctx', 'head')), may hold values from -3 to 3
Outputs:
- query_grad: float32 [8192, 2048], P('ctx', 'head')
- key_grad: float32 [8192, 1024], P('ctx', 'head')
- value_grad: float32 [8192, 1024], P('ctx', 'head')
- weight_grad: float32 [128, 16, 4608], P('ctx', 'head')
The draws below stay inside these ranges and needn't reach their ends.
All inputs are finite; a program needn't handle non-finite values.
Results may differ from the reference program's by a relative error of at most 0.02.
Values may be sent and summed in bfloat16 or wider, within the bound.
A program may use at most 128 MiB of HBM per device.

```python
import math
import jax
import jax.numpy as jnp
from jax import lax

D = 4608
HQ = 16
HK = 8
HD = 128
WINDOW = 4096
TOK_DEV = 512
SPAN = 8
TOKENS = 8192


def draw_queries(key, part):
    first_key, second_key = jax.random.split(jax.random.fold_in(key, 17))
    base = jnp.clip(jax.random.normal(first_key, (TOKENS, HQ, HD), jnp.float32), -6.0, 6.0)
    scales = jnp.exp(jax.random.uniform(second_key, (TOKENS, HQ, 1), jnp.float32, math.log(0.5), math.log(4.0)))
    return (base * scales).reshape(TOKENS, HQ * HD).astype(jnp.bfloat16)


def level_of(rng, shape, pieces, least, high):
    def one(dim, blocks):
        draws = jax.random.uniform(jax.random.fold_in(jax.random.fold_in(rng, 6), dim), (blocks,), jnp.float32, least / len(pieces), high / len(pieces))
        return jnp.repeat(jnp.exp(draws), shape[dim] // blocks).reshape((-1,) + (1,) * (len(shape) - dim - 1))

    loudness = one(*pieces[0])
    for cut in pieces[1:]:
        loudness = loudness * one(*cut)
    return loudness


def gaussian(own_key, extent, spread, bound, cuts=(), held_as=jnp.bfloat16):
    values = spread * jax.random.normal(own_key, extent, jnp.float32)
    if cuts:
        values = values * level_of(own_key, extent, cuts, -0.22, 0.18)
    return jnp.clip(values, -bound, bound).astype(held_as)


def setup_inputs(seed: int = 0) -> dict:
    splits = jax.random.split(jax.random.key(seed), 6)
    queries = draw_queries(jax.random.fold_in(splits[5], 71), 0)
    keys = gaussian(splits[1], (TOKENS, HK * HD), 1.0, 6.0, ((0, 16), (1, 2)))
    values = gaussian(splits[2], (TOKENS, HK * HD), 1.0, 6.0, ((0, 16), (1, 2)))
    out_weight = gaussian(splits[3], (HD, HQ, D), (HQ * HD) ** -0.5, 0.125, ((1, 2),))
    cotangent = gaussian(splits[4], (TOKENS, D), 0.5, 3.0, ((0, 32),))
    return dict(queries=queries, keys=keys, values=values, out_weight=out_weight, cotangent=cotangent)


SOFT_CAP = 50.0
QUERY_MULTIPLIER = 144.0 ** -0.5
ROPE_BASE = 10000.0


def rotary_tables(positions, width):
    half_width = width // 2
    frequency = ROPE_BASE ** (-(jnp.arange(half_width, dtype=jnp.float32) * 2.0) / width)
    angles = positions.astype(jnp.float32)[:, None] * frequency[None, :]
    return jnp.cos(angles)[:, None, :], jnp.sin(angles)[:, None, :]


def rotate(values_in, cosine, sine_table):
    half_width = values_in.shape[-1] // 2
    first_half = values_in[..., :half_width]
    second_half = values_in[..., half_width:]
    return jnp.concatenate([first_half * cosine - second_half * sine_table, second_half * cosine + first_half * sine_table], axis=-1)


def unrotate(values_in, cosine, sine_table):
    half_width = values_in.shape[-1] // 2
    first_half = values_in[..., :half_width]
    second_half = values_in[..., half_width:]
    return jnp.concatenate([first_half * cosine + second_half * sine_table, second_half * cosine - first_half * sine_table], axis=-1)


def return_journey(values_in):
    return lax.optimization_barrier(values_in.astype(jnp.bfloat16)).astype(jnp.float32)


def reference(queries, keys, values, out_weight, cotangent):
    group_size = HQ // HK
    block = TOK_DEV
    blocks_all = TOKENS // block
    padding = SPAN * block
    width_keys = (SPAN + 1) * block
    positions = jnp.arange(TOKENS, dtype=jnp.int32)
    cosine, sine_table = rotary_tables(positions, HD)
    query_rotated = return_journey(rotate(queries.reshape(TOKENS, HQ, HD).astype(jnp.float32), cosine, sine_table)).reshape(TOKENS, HK, group_size, HD)
    key_rot = return_journey(rotate(keys.reshape(TOKENS, HK, HD).astype(jnp.float32), cosine, sine_table))
    value_all = values.reshape(TOKENS, HK, HD).astype(jnp.float32)
    output_gradient = return_journey(jnp.einsum("td,ehd->the", cotangent.astype(jnp.float32), out_weight.astype(jnp.float32))).reshape(TOKENS, HK, group_size, HD)
    key_pad = jnp.concatenate([jnp.zeros((padding, HK, HD), jnp.float32), key_rot], axis=0)
    value_pad = jnp.concatenate([jnp.zeros((padding, HK, HD), jnp.float32), value_all], axis=0)

    def one_block(state, block_index):
        key_grad_all, value_grad_all = state
        first = block_index * block
        query_block = lax.dynamic_slice_in_dim(query_rotated, first, block, 0)
        gradient_block = lax.dynamic_slice_in_dim(output_gradient, first, block, 0)
        key_window_rows = lax.dynamic_slice_in_dim(key_pad, first, width_keys, 0)
        value_window_rows = lax.dynamic_slice_in_dim(value_pad, first, width_keys, 0)
        query_pos = first + jnp.arange(block, dtype=jnp.int32)
        key_pos = first - padding + jnp.arange(width_keys, dtype=jnp.int32)
        offset = query_pos[:, None] - key_pos[None, :]
        visible = (offset >= 0) & (offset < WINDOW) & (key_pos[None, :] >= 0)
        uncapped_score = jnp.einsum("qfwy,vfy->fwqv", query_block, key_window_rows) * QUERY_MULTIPLIER
        tanh_val = jnp.tanh(uncapped_score / SOFT_CAP)
        capped = SOFT_CAP * tanh_val
        exponent_score = jnp.where(visible, jnp.exp(capped), 0.0)
        row_total = jnp.sum(exponent_score, axis=-1)
        weighted_values = jnp.einsum("fpxe,efv->xfpv", return_journey(exponent_score), value_window_rows)
        attn_blk = return_journey(weighted_values / jnp.transpose(row_total, (2, 0, 1))[..., None])
        log_total = jnp.log(row_total)
        row_delta = jnp.transpose(jnp.sum(gradient_block * attn_blk, axis=-1), (1, 2, 0))
        softmax_probability = jnp.where(visible, jnp.exp(capped - log_total[..., None]), 0.0)
        probability_gradient = jnp.einsum("qfwy,vfy->fwqv", gradient_block, value_window_rows)
        score_gradient = return_journey(softmax_probability * (probability_gradient - row_delta[..., None]) * (1.0 - tanh_val * tanh_val) * QUERY_MULTIPLIER)
        query_portion = jnp.einsum("fpxe,efv->xfpv", score_gradient, key_window_rows)
        key_portion = jnp.einsum("vcfh,fvcx->hvx", score_gradient, query_block)
        value_portion = jnp.einsum("vcfh,fvcx->hvx", return_journey(softmax_probability), gradient_block)
        key_grad_all = lax.dynamic_update_slice_in_dim(key_grad_all, lax.dynamic_slice_in_dim(key_grad_all, first, width_keys, 0) + key_portion, first, 0)
        value_grad_all = lax.dynamic_update_slice_in_dim(value_grad_all, lax.dynamic_slice_in_dim(value_grad_all, first, width_keys, 0) + value_portion, first, 0)
        return (key_grad_all, value_grad_all), (query_portion, attn_blk)

    start_state = (jnp.zeros((padding + TOKENS, HK, HD), jnp.float32), jnp.zeros((padding + TOKENS, HK, HD), jnp.float32))
    (key_grad_all, value_grad_all), (query_parts, attn_parts) = lax.scan(one_block, start_state, jnp.arange(blocks_all, dtype=jnp.int32))
    query_grad = unrotate(query_parts.reshape(TOKENS, HQ, HD), cosine, sine_table).reshape(TOKENS, HQ * HD)
    key_grad = unrotate(key_grad_all[padding:], cosine, sine_table).reshape(TOKENS, HK * HD)
    value_grad = value_grad_all[padding:].reshape(TOKENS, HK * HD)
    attn_all = attn_parts.reshape(TOKENS, HQ, HD)
    weight_grad = jnp.einsum("the,td->ehd", attn_all, cotangent.astype(jnp.float32))
    return (query_grad, key_grad, value_grad, weight_grad)
```

```python
import functools

import jax
import jax.numpy as jnp
from jax import lax
from jax.experimental import pallas as pl
from jax.experimental.pallas import tpu as pltpu
from jax.sharding import PartitionSpec as P

SPAN = 8
SOFT_CAP = 50.0
QUERY_MULTIPLIER = 144.0 ** (-0.5)
ROPE_BASE = 10000.0
LOG2E = 1.4426950408889634
F32, BF16 = jnp.float32, jnp.bfloat16
NT = (((1,), (1,)), ((), ()))
NN = (((1,), (0,)), ((), ()))


def dot(a, b, dims=NN):
    return lax.dot_general(a, b, dims, preferred_element_type=F32)


def rotary_tables(positions, width):
    half_width = width // 2
    frequency = ROPE_BASE ** (-(jnp.arange(half_width, dtype=jnp.float32) * 2.0) / width)
    angles = positions.astype(jnp.float32)[:, None] * frequency[None, :]
    return (jnp.cos(angles)[:, None, :], jnp.sin(angles)[:, None, :])


def rotate(values_in, cosine, sine):
    half = values_in.shape[-1] // 2
    a, b = values_in[..., :half], values_in[..., half:]
    return jnp.concatenate([a * cosine - b * sine, b * cosine + a * sine], axis=-1)


def tanh_of(scores):
    return jnp.tanh(scores * (QUERY_MULTIPLIER / SOFT_CAP))


def exp_of(th):
    return jnp.exp2(th * (SOFT_CAP * LOG2E))


def fwd_kernel(tok, hd, heads, start_ref, q_ref, kv_ref, attn_ref, linv_ref, acc_ref):
    i = pl.program_id(0)
    j0 = start_ref[0]
    row = lax.broadcasted_iota(jnp.int32, (tok, tok), 0)
    col = lax.broadcasted_iota(jnp.int32, (tok, tok), 1)

    def tile(j, mask, first):
        rows = pl.ds(pl.multiple_of(j * tok, tok), tok)
        k = kv_ref[rows, 0:hd]
        vx = kv_ref[rows, hd : 3 * hd]
        for h in range(heads):
            s = dot(q_ref[:, h * hd : (h + 1) * hd], k, NT)
            e = exp_of(tanh_of(s))
            if mask is not None:
                e = jnp.where(mask, e, 0.0)
            part = dot(e.astype(BF16), vx)
            if first:
                acc_ref[h] = part
            else:
                acc_ref[h] += part

    tile(i + SPAN, row >= col, True)

    def mid(j, carry):
        tile(j, None, False)
        return carry

    lax.fori_loop(jnp.maximum(i + 1, j0), i + SPAN, mid, 0)

    @pl.when(i >= j0)
    def _():
        tile(i, row < col, False)

    for h in range(heads):
        total = acc_ref[h, :, hd : 2 * hd]
        inv = 1.0 / total
        cols = slice(h * hd, (h + 1) * hd)
        attn_ref[:, cols] = (acc_ref[h, :, 0:hd] * inv).astype(BF16)
        linv_ref[:, cols] = inv


def bwd_kernel(
    tok, hd, heads, start_ref, q_ref, attn_ref, linv_ref, do_ref, kv_ref, kt_ref,
    gq_ref, gkv_ref, qs_ref, dos_ref, dox_ref, dqt_ref,
):
    i = pl.program_id(0)
    j0 = start_ref[0]
    key = lax.broadcasted_iota(jnp.int32, (tok, tok), 0)
    qry = lax.broadcasted_iota(jnp.int32, (tok, tok), 1)

    @pl.when(i == 0)
    def _():
        gkv_ref[...] = jnp.zeros_like(gkv_ref)

    lane = lax.broadcasted_iota(jnp.int32, (tok, hd), 1)
    for h in range(heads):
        cols = slice(h * hd, (h + 1) * hd)
        inv = linv_ref[:, cols]
        do = do_ref[:, cols]
        dof = do.astype(F32)
        qs_ref[:, cols] = (q_ref[:, cols].astype(F32) * (inv * QUERY_MULTIPLIER)).astype(BF16)
        dos_ref[:, cols] = (dof * inv).astype(BF16)
        delta = jnp.sum(dof * attn_ref[:, cols].astype(F32), axis=-1, keepdims=True)
        delta = jnp.broadcast_to(-delta, (tok, hd))
        hi = delta.astype(BF16).astype(F32)
        lo = (delta - hi).astype(BF16).astype(F32)
        lo2 = delta - hi - lo
        packed = jnp.where(
            lane == 0, hi, jnp.where(lane == 1, lo, jnp.where(lane == 2, lo2, 0.0))
        )
        dox_ref[h, :, 0:hd] = do
        dox_ref[h, :, hd : 2 * hd] = packed.astype(BF16)

    def tile(j, mask, first):
        rows = pl.ds(pl.multiple_of(j * tok, tok), tok)
        k = kv_ref[rows, 0:hd]
        vx = kv_ref[rows, hd : 3 * hd]
        kt = kt_ref[:, rows]
        gk = None
        for h in range(heads):
            cols = slice(h * hd, (h + 1) * hd)
            th = tanh_of(dot(k, q_ref[:, cols], NT))
            e = exp_of(th)
            if mask is not None:
                e = jnp.where(mask, e, 0.0)
            dp = dot(vx, dox_ref[h], NT)
            ds = (e * (1.0 - th * th) * dp).astype(BF16)
            part_v = dot(e.astype(BF16), dos_ref[:, cols])
            part_k = dot(ds, qs_ref[:, cols])
            part_q = dot(kt, ds)
            if first:
                dqt_ref[h] = part_q
            else:
                dqt_ref[h] += part_q
            gk = part_k if gk is None else gk + part_k
            gv = part_v if h == 0 else gv + part_v
        gkv_ref[rows, 0:hd] += gk
        gkv_ref[rows, hd : 2 * hd] += gv

    tile(i + SPAN, qry >= key, True)

    def mid(j, carry):
        tile(j, None, False)
        return carry

    lax.fori_loop(jnp.maximum(i + 1, j0), i + SPAN, mid, 0)

    @pl.when(i >= j0)
    def _():
        tile(i, qry < key, False)

    for h in range(heads):
        cols = slice(h * hd, (h + 1) * hd)
        gq = dqt_ref[h].T * (linv_ref[:, cols] * QUERY_MULTIPLIER)
        gq_ref[:, cols] = gq.astype(BF16)


def local(queries, keys, values, out_weight, cotangent):
    tok = queries.shape[0]
    hd = out_weight.shape[0]
    nq = queries.shape[1] // hd
    group = keys.shape[1] // hd
    heads = nq // group
    n_ctx = lax.axis_size("ctx")
    n_head = lax.axis_size("head")
    hops = SPAN // group
    me = lax.axis_index("ctx")
    rank = me % group
    chunk = group * tok

    def exchange(payload):
        out = jnp.zeros_like(payload)
        own = lax.dynamic_index_in_dim(payload, rank, 0)
        out = lax.dynamic_update_slice_in_dim(out, own, rank, 0)
        for d in range(1, group):
            piece = lax.dynamic_index_in_dim(payload, (rank + d) % group, 0)
            route = [(s, s - s % group + (s % group + d) % group) for s in range(n_ctx)]
            got = lax.ppermute(piece, "ctx", route)
            out = lax.dynamic_update_slice_in_dim(out, got, (rank - d) % group, 0)
        return out

    def shift(block, by):
        route = [(s, s + by) for s in range(n_ctx) if 0 <= s + by < n_ctx]
        return lax.ppermute(block, "ctx", route)

    if n_head == 2:
        other = lax.ppermute(cotangent, "head", [(0, 1), (1, 0)])
        first = lax.axis_index("head") == 0
        full_grad = jnp.concatenate(
            [jnp.where(first, cotangent, other), jnp.where(first, other, cotangent)], axis=0
        )
    else:
        full_grad = lax.all_gather(cotangent, "head", axis=0, tiled=True)

    positions = me * tok + jnp.arange(tok, dtype=jnp.int32)
    cosine, sine = rotary_tables(positions, hd)
    qr = rotate(queries.reshape(tok, nq, hd).astype(F32), cosine, sine).astype(BF16)
    kr = rotate(keys.reshape(tok, group, hd).astype(F32), cosine, sine).astype(BF16)
    payload = jnp.concatenate(
        [qr.reshape(tok, group, heads * hd), kr, values.reshape(tok, group, hd)], axis=-1
    ).transpose(1, 0, 2)
    mine = exchange(payload).reshape(chunk, (heads + 2) * hd)
    q_own = mine[:, : heads * hd]
    window = [mine[:, heads * hd :]]
    for _ in range(hops):
        window.insert(0, shift(window[0], group))
    kv = jnp.concatenate(window, axis=0)
    kv_rows = kv.shape[0]
    kv = jnp.concatenate([kv, jnp.ones((kv_rows, hd), BF16)], axis=1)
    start = jnp.maximum(0, SPAN - (me // group) * group).astype(jnp.int32).reshape(1)

    width = heads * hd
    smem = pl.BlockSpec(memory_space=pltpu.SMEM)
    by_query = pl.BlockSpec((tok, width), lambda i: (i, 0))
    kv_spec = pl.BlockSpec((kv_rows, 3 * hd), lambda i: (0, 0))
    pairs = chunk * heads * SPAN * tok
    attn, linv = pl.pallas_call(
        functools.partial(fwd_kernel, tok, hd, heads),
        grid=(group,),
        out_shape=(
            jax.ShapeDtypeStruct((chunk, width), BF16),
            jax.ShapeDtypeStruct((chunk, width), F32),
        ),
        in_specs=[smem, by_query, kv_spec],
        out_specs=(by_query, by_query),
        scratch_shapes=[pltpu.VMEM((heads, tok, 2 * hd), F32)],
        compiler_params=pltpu.CompilerParams(vmem_limit_bytes=56 * 2**20),
        cost_estimate=pl.CostEstimate(
            flops=8 * pairs * hd, bytes_accessed=8 * 2**20, transcendentals=2 * pairs
        ),
        name="attend",
    )(start, q_own, kv)

    dout = jnp.einsum("td,ehd->the", full_grad, out_weight, preferred_element_type=F32)
    dout = dout.astype(BF16).reshape(tok, group, width).transpose(1, 0, 2)
    dout_own = exchange(dout).reshape(chunk, width)

    attn_tok = exchange(attn.reshape(group, tok, width)).transpose(1, 0, 2).reshape(tok, nq, hd)
    term = jnp.einsum("the,td->ehd", attn_tok, full_grad, preferred_element_type=F32)
    term = term.astype(BF16).reshape(n_ctx, hd // n_ctx, nq, full_grad.shape[1])
    bit = 1
    while bit < n_ctx:
        term = term.reshape(term.shape[0] // 2, 2, *term.shape[1:])
        mine_bit = (me // bit) % 2
        keep = lax.dynamic_index_in_dim(term, mine_bit, 1, keepdims=False)
        send = lax.dynamic_index_in_dim(term, 1 - mine_bit, 1, keepdims=False)
        got = lax.ppermute(send, "ctx", [(s, s ^ bit) for s in range(n_ctx)])
        total = keep.astype(F32) + got.astype(F32)
        bit *= 2
        term = total.astype(BF16) if bit < n_ctx else total
    weight_grad = term[0]

    kt = kv[:, 0:hd].T
    gq, gkv = pl.pallas_call(
        functools.partial(bwd_kernel, tok, hd, heads),
        grid=(group,),
        out_shape=(
            jax.ShapeDtypeStruct((chunk, width), BF16),
            jax.ShapeDtypeStruct((kv_rows, 2 * hd), F32),
        ),
        in_specs=[
            smem, by_query, by_query, by_query, by_query, kv_spec,
            pl.BlockSpec((hd, kv_rows), lambda i: (0, 0)),
        ],
        out_specs=(by_query, pl.BlockSpec((kv_rows, 2 * hd), lambda i: (0, 0))),
        scratch_shapes=[
            pltpu.VMEM((tok, width), BF16),
            pltpu.VMEM((tok, width), BF16),
            pltpu.VMEM((heads, tok, 2 * hd), BF16),
            pltpu.VMEM((heads, hd, tok), F32),
        ],
        compiler_params=pltpu.CompilerParams(vmem_limit_bytes=56 * 2**20),
        cost_estimate=pl.CostEstimate(
            flops=20 * pairs * hd, bytes_accessed=20 * 2**20, transcendentals=2 * pairs
        ),
        name="attend_grad",
    )(start, q_own, attn, linv, dout_own, kv, kt)

    parts = gkv.reshape(hops + 1, chunk, 2 * hd)
    running = parts[0]
    for step in range(hops):
        running = shift(running.astype(BF16), -group).astype(F32) + parts[step + 1]
    gq_tok = exchange(gq.reshape(group, tok, width)).transpose(1, 0, 2)
    gkv_tok = exchange(running.astype(BF16).reshape(group, tok, 2 * hd)).transpose(1, 0, 2)
    query_grad = rotate(gq_tok.reshape(tok, nq, hd).astype(F32), cosine, -sine)
    key_grad = rotate(gkv_tok[..., :hd].astype(F32), cosine, -sine)
    value_grad = gkv_tok[..., hd:].astype(F32)
    return (
        query_grad.reshape(tok, nq * hd),
        key_grad.reshape(tok, group * hd),
        value_grad.reshape(tok, group * hd),
        weight_grad,
    )


def solution(mesh):
    placed = (
        P("ctx", "head"),
        P("ctx", "head"),
        P("ctx", "head"),
        P(None, "head", None),
        P(("ctx", "head"), None),
    )
    return jax.shard_map(
        local,
        mesh=mesh,
        in_specs=placed,
        out_specs=(P("ctx", "head"), P("ctx", "head"), P("ctx", "head"), P("ctx", "head", None)),
        check_vma=False,
    )
```

```python
import functools

import jax
import jax.numpy as jnp
from jax import lax
from jax.experimental import pallas as pl
from jax.experimental.pallas import tpu as pltpu
from jax.sharding import PartitionSpec as P

SPAN = 8
SOFT_CAP = 50.0
QUERY_MULTIPLIER = 144.0 ** (-0.5)
ROPE_BASE = 10000.0
LOG2E = 1.4426950408889634
F32, BF16 = jnp.float32, jnp.bfloat16
NT = (((1,), (1,)), ((), ()))
NN = (((1,), (0,)), ((), ()))


def dot(a, b, dims=NN):
    return lax.dot_general(a, b, dims, preferred_element_type=F32)


def rotary_tables(positions, width):
    half_width = width // 2
    frequency = ROPE_BASE ** (-(jnp.arange(half_width, dtype=jnp.float32) * 2.0) / width)
    angles = positions.astype(jnp.float32)[:, None] * frequency[None, :]
    return (jnp.cos(angles)[:, None, :], jnp.sin(angles)[:, None, :])


def rotate(values_in, cosine, sine):
    half = values_in.shape[-1] // 2
    a, b = values_in[..., :half], values_in[..., half:]
    return jnp.concatenate([a * cosine - b * sine, b * cosine + a * sine], axis=-1)


def tanh_of(scores):
    return jnp.tanh(scores * (QUERY_MULTIPLIER / SOFT_CAP))


def exp_of(th):
    return jnp.exp2(th * (SOFT_CAP * LOG2E))


def fwd_kernel(tok, hd, heads, start_ref, q_ref, kv_ref, attn_ref, linv_ref, acc_ref):
    i = pl.program_id(0)
    j0 = start_ref[0]
    row = lax.broadcasted_iota(jnp.int32, (tok, tok), 0)
    col = lax.broadcasted_iota(jnp.int32, (tok, tok), 1)

    def tile(j, mask, first):
        rows = pl.ds(pl.multiple_of(j * tok, tok), tok)
        k = kv_ref[rows, 0:hd]
        vx = kv_ref[rows, hd : 3 * hd]
        for h in range(heads):
            s = dot(q_ref[:, h * hd : (h + 1) * hd], k, NT)
            e = exp_of(tanh_of(s))
            if mask is not None:
                e = jnp.where(mask, e, 0.0)
            part = dot(e.astype(BF16), vx)
            if first:
                acc_ref[h] = part
            else:
                acc_ref[h] += part

    tile(i + SPAN, row >= col, True)

    def mid(j, carry):
        tile(j, None, False)
        return carry

    lax.fori_loop(jnp.maximum(i + 1, j0), i + SPAN, mid, 0)

    @pl.when(i >= j0)
    def _():
        tile(i, row < col, False)

    for h in range(heads):
        total = acc_ref[h, :, hd : 2 * hd]
        inv = 1.0 / total
        cols = slice(h * hd, (h + 1) * hd)
        attn_ref[:, cols] = (acc_ref[h, :, 0:hd] * inv).astype(BF16)
        linv_ref[:, cols] = inv


def bwd_kernel(
    tok, hd, heads, group, part, low, diag, start_ref, q_ref, attn_ref, linv_ref, do_ref,
    kv_ref, gq_ref, gkv_ref, qs_ref, dos_ref, dox_ref, dqt_ref, kt_ref,
):
    i = pl.program_id(0)
    j0 = jnp.maximum(start_ref[0] - part * group, 0)
    key = lax.broadcasted_iota(jnp.int32, (tok, tok), 0)
    qry = lax.broadcasted_iota(jnp.int32, (tok, tok), 1)

    @pl.when(i == 0)
    def _():
        gkv_ref[...] = jnp.zeros_like(gkv_ref)
        for j in range(group):
            rows = slice(j * tok, (j + 1) * tok)
            kt_ref[:, rows] = kv_ref[rows, 0:hd].astype(F32).T.astype(BF16)

    dqt_ref[...] = jnp.zeros_like(dqt_ref)
    lane = lax.broadcasted_iota(jnp.int32, (tok, hd), 1)
    for h in range(heads):
        cols = slice(h * hd, (h + 1) * hd)
        inv = linv_ref[:, cols]
        do = do_ref[:, cols]
        dof = do.astype(F32)
        qs_ref[:, cols] = (q_ref[:, cols].astype(F32) * (inv * QUERY_MULTIPLIER)).astype(BF16)
        dos_ref[:, cols] = (dof * inv).astype(BF16)
        delta = jnp.sum(dof * attn_ref[:, cols].astype(F32), axis=-1, keepdims=True)
        delta = jnp.broadcast_to(-delta, (tok, hd))
        hi = delta.astype(BF16).astype(F32)
        lo = (delta - hi).astype(BF16).astype(F32)
        lo2 = delta - hi - lo
        packed = jnp.where(
            lane == 0, hi, jnp.where(lane == 1, lo, jnp.where(lane == 2, lo2, 0.0))
        )
        dox_ref[h, :, 0:hd] = do
        dox_ref[h, :, hd : 2 * hd] = packed.astype(BF16)

    def tile(j, mask):
        rows = pl.ds(pl.multiple_of(j * tok, tok), tok)
        k = kv_ref[rows, 0:hd]
        vx = kv_ref[rows, hd : 3 * hd]
        kt = kt_ref[:, rows]
        gk = None
        for h in range(heads):
            cols = slice(h * hd, (h + 1) * hd)
            th = tanh_of(dot(k, q_ref[:, cols], NT))
            e = exp_of(th)
            if mask is not None:
                e = jnp.where(mask, e, 0.0)
            dp = dot(vx, dox_ref[h], NT)
            ds = (e * (1.0 - th * th) * dp).astype(BF16)
            part_v = dot(e.astype(BF16), dos_ref[:, cols])
            part_k = dot(ds, qs_ref[:, cols])
            part_q = dot(kt, ds)
            dqt_ref[h] += part_q
            gk = part_k if gk is None else gk + part_k
            gv = part_v if h == 0 else gv + part_v
        gkv_ref[rows, 0:hd] += gk
        gkv_ref[rows, hd : 2 * hd] += gv

    if diag:
        tile(i, qry >= key)

    def mid(j, carry):
        tile(j, None)
        return carry

    lax.fori_loop(jnp.maximum(i + 1, j0) if low else j0, i if diag else group, mid, 0)

    if low:

        @pl.when(i >= j0)
        def _():
            tile(i, qry < key)

    for h in range(heads):
        cols = slice(h * hd, (h + 1) * hd)
        gq = dqt_ref[h].T * (linv_ref[:, cols] * QUERY_MULTIPLIER)
        gq_ref[:, cols] = gq


def local(queries, keys, values, out_weight, cotangent):
    tok = queries.shape[0]
    hd = out_weight.shape[0]
    nq = queries.shape[1] // hd
    group = keys.shape[1] // hd
    heads = nq // group
    n_ctx = lax.axis_size("ctx")
    n_head = lax.axis_size("head")
    hops = SPAN // group
    me = lax.axis_index("ctx")
    rank = me % group
    chunk = group * tok

    def exchange(payload):
        out = jnp.zeros_like(payload)
        own = lax.dynamic_index_in_dim(payload, rank, 0)
        out = lax.dynamic_update_slice_in_dim(out, own, rank, 0)
        for d in range(1, group):
            piece = lax.dynamic_index_in_dim(payload, (rank + d) % group, 0)
            route = [(s, s - s % group + (s % group + d) % group) for s in range(n_ctx)]
            got = lax.ppermute(piece, "ctx", route)
            out = lax.dynamic_update_slice_in_dim(out, got, (rank - d) % group, 0)
        return out

    def shift(block, by):
        route = [(s, s + by) for s in range(n_ctx) if 0 <= s + by < n_ctx]
        return lax.ppermute(block, "ctx", route)

    if n_head == 2:
        other = lax.ppermute(cotangent, "head", [(0, 1), (1, 0)])
        first = lax.axis_index("head") == 0
        full_grad = jnp.concatenate(
            [jnp.where(first, cotangent, other), jnp.where(first, other, cotangent)], axis=0
        )
    else:
        full_grad = lax.all_gather(cotangent, "head", axis=0, tiled=True)

    positions = me * tok + jnp.arange(tok, dtype=jnp.int32)
    cosine, sine = rotary_tables(positions, hd)
    qr = rotate(queries.reshape(tok, nq, hd).astype(F32), cosine, sine).astype(BF16)
    kr = rotate(keys.reshape(tok, group, hd).astype(F32), cosine, sine).astype(BF16)
    payload = jnp.concatenate(
        [qr.reshape(tok, group, heads * hd), kr, values.reshape(tok, group, hd)], axis=-1
    ).transpose(1, 0, 2)
    mine = exchange(payload).reshape(chunk, (heads + 2) * hd)
    q_own = mine[:, : heads * hd]
    window = [mine[:, heads * hd :]]
    for _ in range(hops):
        window.insert(0, shift(window[0], group))
    kv = jnp.concatenate(window, axis=0)
    kv_rows = kv.shape[0]
    kv = jnp.concatenate([kv, jnp.ones((kv_rows, hd), BF16)], axis=1)
    start = jnp.maximum(0, SPAN - (me // group) * group).astype(jnp.int32).reshape(1)

    width = heads * hd
    smem = pl.BlockSpec(memory_space=pltpu.SMEM)
    by_query = pl.BlockSpec((tok, width), lambda i: (i, 0))
    kv_spec = pl.BlockSpec((kv_rows, 3 * hd), lambda i: (0, 0))
    pairs = chunk * heads * SPAN * tok
    attn, linv = pl.pallas_call(
        functools.partial(fwd_kernel, tok, hd, heads),
        grid=(group,),
        out_shape=(
            jax.ShapeDtypeStruct((chunk, width), BF16),
            jax.ShapeDtypeStruct((chunk, width), F32),
        ),
        in_specs=[smem, by_query, kv_spec],
        out_specs=(by_query, by_query),
        scratch_shapes=[pltpu.VMEM((heads, tok, 2 * hd), F32)],
        compiler_params=pltpu.CompilerParams(vmem_limit_bytes=56 * 2**20),
        cost_estimate=pl.CostEstimate(
            flops=8 * pairs * hd, bytes_accessed=8 * 2**20, transcendentals=2 * pairs
        ),
        name="attend",
    )(start, q_own, kv)

    dout = jnp.einsum("td,ehd->the", full_grad, out_weight, preferred_element_type=F32)
    dout = dout.astype(BF16).reshape(tok, group, width).transpose(1, 0, 2)
    dout_own = exchange(dout).reshape(chunk, width)

    attn_tok = exchange(attn.reshape(group, tok, width)).transpose(1, 0, 2).reshape(tok, nq, hd)
    term = jnp.einsum("the,td->ehd", attn_tok, full_grad, preferred_element_type=F32)
    term = term.astype(BF16).reshape(n_ctx, hd // n_ctx, nq, full_grad.shape[1])
    bit = 1
    while bit < n_ctx:
        term = term.reshape(term.shape[0] // 2, 2, *term.shape[1:])
        mine_bit = (me // bit) % 2
        keep = lax.dynamic_index_in_dim(term, mine_bit, 1, keepdims=False)
        send = lax.dynamic_index_in_dim(term, 1 - mine_bit, 1, keepdims=False)
        got = lax.ppermute(send, "ctx", [(s, s ^ bit) for s in range(n_ctx)])
        total = keep.astype(F32) + got.astype(F32)
        bit *= 2
        term = total.astype(BF16) if bit < n_ctx else total
    weight_grad = term[0]

    chunk_spec = pl.BlockSpec((chunk, 3 * hd), lambda i: (0, 0))
    gq = None
    running = None
    for part in range(hops + 1):
        low, diag = part == 0, part == hops
        share = (group + 1) / (2 * group) if low or diag else 1.0
        gq_part, gkv = pl.pallas_call(
            functools.partial(bwd_kernel, tok, hd, heads, group, part, low, diag),
            grid=(group,),
            out_shape=(
                jax.ShapeDtypeStruct((chunk, width), F32),
                jax.ShapeDtypeStruct((chunk, 2 * hd), F32),
            ),
            in_specs=[smem, by_query, by_query, by_query, by_query, chunk_spec],
            out_specs=(by_query, pl.BlockSpec((chunk, 2 * hd), lambda i: (0, 0))),
            scratch_shapes=[
                pltpu.VMEM((tok, width), BF16),
                pltpu.VMEM((tok, width), BF16),
                pltpu.VMEM((heads, tok, 2 * hd), BF16),
                pltpu.VMEM((heads, hd, tok), F32),
                pltpu.VMEM((hd, chunk), BF16),
            ],
            compiler_params=pltpu.CompilerParams(vmem_limit_bytes=48 * 2**20),
            cost_estimate=pl.CostEstimate(
                flops=int(40 * chunk * chunk * heads * hd * share),
                bytes_accessed=12 * 2**20,
                transcendentals=int(2 * chunk * chunk * heads * share),
            ),
            name="attend_grad",
        )(start, q_own, attn, linv, dout_own, kv[part * chunk : (part + 1) * chunk])
        gq = gq_part if gq is None else gq + gq_part
        if running is not None:
            gkv = gkv + shift(running, -group).astype(F32)
        running = gkv.astype(BF16)
    gq = gq.astype(BF16)
    gq_tok = exchange(gq.reshape(group, tok, width)).transpose(1, 0, 2)
    gkv_tok = exchange(running.reshape(group, tok, 2 * hd)).transpose(1, 0, 2)
    query_grad = rotate(gq_tok.reshape(tok, nq, hd).astype(F32), cosine, -sine)
    key_grad = rotate(gkv_tok[..., :hd].astype(F32), cosine, -sine)
    value_grad = gkv_tok[..., hd:].astype(F32)
    return (
        query_grad.reshape(tok, nq * hd),
        key_grad.reshape(tok, group * hd),
        value_grad.reshape(tok, group * hd),
        weight_grad,
    )


def solution(mesh):
    placed = (
        P("ctx", "head"),
        P("ctx", "head"),
        P("ctx", "head"),
        P(None, "head", None),
        P(("ctx", "head"), None),
    )
    return jax.shard_map(
        local,
        mesh=mesh,
        in_specs=placed,
        out_specs=(P("ctx", "head"), P("ctx", "head"), P("ctx", "head"), P("ctx", "head", None)),
        check_vma=False,
    )
```
